32 devices in a mesh: patch: 16 (over z, y, x), stream: 2 (over core).
Axes of the slice: x: 2, y: 2, z: 4, core: 2. Of those that a mesh axis runs over, the one named last changes fastest.
Arguments:
- exposures: bfloat16 [4, 2, 256, 8, 4096], P(None, 'stream', 'patch'), may hold values from -6 to 6
- owners: int32 [4, 2, 256, 2], P(None, 'stream', 'patch'), may hold values from 0 to 15, all different within a row; in each aligned block of 16 rows (0 to 15, 16 to 31, ..., all dimensions but the last counted through in order) at most 2 rows name the same one
- offsets: int32 [4, 2, 256, 2], P(None, 'stream', 'patch'), may hold values from 0 to 56
- visit_shift: float32 [4, 2, 2], P(None, 'stream'), may hold values from 0.05 to 0.95
- visit_weight: float32 [4, 2], P(None, 'stream'), may hold values from 0.25 to 4
- psf_class: int32 [4, 2], P(None, 'stream'), may hold values from 0 to 7
- coef_table: float32 [8, 16], replicated, may hold values from -0.18 to 0.18
- basis_x: float32 [16, 31], replicated, may hold values from -1 to 1
- basis_y: float32 [16, 31], replicated, may hold values from -1 to 1
Outputs:
- coadd: float32 [1024, 4096], P(('patch', 'stream'))
The draws below stay inside these ranges and needn't reach their ends.
Inputs may be any that keep to these rules, and one draw needn't show every extreme that they name: `owners`: each row names 2 different patches; in each step the 16 strips of one holder name one patch at most 2 times, a bound that some block reaches.
All inputs are finite; a program needn't handle non-finite values.
Results may differ from the reference program's by a relative error of at most 0.0062.
Values may be sent and summed in bfloat16 or wider, within the bound.
A program may use at most 128 MiB of HBM per device.

```python
import math
import jax
import jax.numpy as jnp
import numpy as np
from jax import lax

COLS = 4096
BASES = 16
TAPS = 31
STRIP_ROWS = 8
FANOUT = 2
CAP = 2
STRIPS = 16
STEPS = 4
CLASSES = 8
SLAB_ROWS = 64
HOLD = 256
N_PATCH = 16
N_STREAM = 2


def plant(result, stream_key, low, high):
    spot = [jax.random.randint(jax.random.fold_in(stream_key, axis), (), 0, length) for axis, length in enumerate(result.shape)]
    longest = result.shape.index(max(result.shape))
    beside = spot[:longest] + [(spot[longest] + 1) % result.shape[longest]] + spot[longest + 1:]
    return result.at[tuple(spot)].set(low).at[tuple(beside)].set(high)


def levels(key, shape, shards, low, largest):
    level, own = 1.0, jax.random.fold_in(key, 6)
    for position, shards_of in shards:
        steps = jnp.exp(jax.random.uniform(jax.random.fold_in(own, position), (shards_of,), jnp.float32, low / len(shards), largest / len(shards)))
        level = level * jnp.repeat(steps, shape[position] // shards_of).reshape([-1 if axis == position else 1 for axis in range(len(shape))])
    return level


def shared_out(stream_key, own, number, rows, number_of, top, limit, lean):
    order = jax.random.permutation(stream_key, number_of)
    packed, ordinary = shares(number_of, rows * top, limit, lean, True), shares(number_of, rows * top, limit, lean, False)
    places = jnp.arange(number_of)

    def named(tallies, turn):
        used = int((tallies > 0).sum())
        fixed = max(1, used // 4)
        moved = fixed + (places - fixed + turn * (used - fixed)) % max(1, number_of - fixed)
        return jnp.zeros((number_of,), jnp.int32).at[order[jnp.where(places < fixed, places, moved)]].set(jnp.asarray(tallies, jnp.int32))

    tallies = jnp.where(number % 4 == 0, named(packed, number // 4), named(ordinary, number - number // 4 - 1))
    mixed = jax.random.permutation(jax.random.fold_in(own, 3), number_of)
    donor, receiver = mixed[0:number_of // 2 * 2:2], mixed[1:number_of // 2 * 2:2]
    margin = jnp.minimum(tallies[donor] - 1, limit - tallies[receiver]) // 2
    margin = jnp.where((donor == order[0]) | (receiver == order[0]) | (tallies[receiver] == 0), 0, jnp.maximum(margin, 0))
    moved = jax.random.randint(jax.random.fold_in(own, 4), (number_of // 2,), 0, 1 << 20) % (margin + 1)
    tallies = tallies.at[donor].add(-moved).at[receiver].add(moved)
    members = jnp.searchsorted(jnp.cumsum(tallies), jnp.arange(rows * top), side="right").astype(jnp.int32)
    table = members.reshape(top, rows).T
    table = table[jax.random.permutation(jax.random.fold_in(own, 1), rows)]
    turn = jax.random.randint(jax.random.fold_in(own, 2), (rows, 1), 0, top)
    return jnp.take_along_axis(table, (jnp.arange(top)[None, :] + turn) % top, axis=1)


def shares(amount, total, most, skew, full):
    loads = [(1 << 20) // math.isqrt(standing ** skew) + 1 for standing in range(1, amount + 1)]
    largest = most if full else min(most, max(-(-total // amount), total * loads[0] // sum(loads)))
    least = 1 if total - largest >= amount - 1 else 0
    holding, spare = [largest] + [least] * (amount - 1), total - largest - least * (amount - 1)
    while spare > 0:
        free = [i for i in range(1, amount) if holding[i] < largest] or [i for i in range(1, amount) if holding[i] < most]
        pool, budget = sum([loads[i] for i in free]), spare
        for i in free:
            extra = min(most - holding[i], max(1, budget * loads[i] // pool), spare)
            holding[i] = holding[i] + extra
            spare = spare - extra
    return np.array(holding)


def bell_draw(stream_key, extent, spread, reach, cuts=(), kind=jnp.bfloat16):
    result = jax.random.normal(stream_key, extent, jnp.float32) * spread
    if len(cuts) > 0:
        result = levels(stream_key, extent, cuts, -0.22, 0.18) * result
    return jnp.clip(result, min=-reach, max=reach).astype(kind)


def setup_inputs(seed: int = 0) -> dict:
    keys = jax.random.split(jax.random.key(seed), 10)
    exposures = bell_draw(keys[0], (STEPS, N_STREAM, HOLD, STRIP_ROWS, COLS), 1.0, 6.0, ((1, 2), (2, 16)))
    owners_keys = jax.random.split(jax.random.fold_in(keys[1], 1), STEPS * N_STREAM * HOLD // STRIPS)
    owners_turns = jax.random.permutation(jax.random.fold_in(keys[1], 3), STEPS * N_STREAM * HOLD // STRIPS)
    owners = jax.vmap(lambda own, number: shared_out(jax.random.fold_in(keys[1], 2), own, number, STRIPS, N_PATCH, FANOUT, CAP, 2))(owners_keys, owners_turns).reshape((STEPS, N_STREAM, HOLD, FANOUT))
    offsets = plant(jax.random.randint(keys[2], (STEPS, N_STREAM, HOLD, FANOUT), 0, SLAB_ROWS - STRIP_ROWS + 1), jax.random.fold_in(keys[2], 1), 0, SLAB_ROWS - STRIP_ROWS).astype(jnp.int32)
    visit_shift = jnp.clip(0.05 + 0.9 * jax.random.uniform(keys[3], (STEPS, N_STREAM, 2), jnp.float32) ** levels(keys[3], (STEPS, N_STREAM, 2), ((1, 2),), -0.2, 0.2), 0.05, 0.95)
    visit_weight = jnp.clip(jnp.exp(math.log(4.0) - 2.7725887 * jax.random.uniform(keys[4], (STEPS, N_STREAM), jnp.float32) ** levels(keys[4], (STEPS, N_STREAM), ((1, 2),), -0.2, 0.2)), 0.25, 4.0)
    psf_class = plant(jax.random.randint(keys[5], (STEPS, N_STREAM), 0, CLASSES), jax.random.fold_in(keys[5], 1), 0, CLASSES - 1).astype(jnp.int32)
    coef_table = bell_draw(keys[6], (CLASSES, BASES), 0.03, 0.18, (), jnp.float32)
    basis_x = bell_draw(keys[7], (BASES, TAPS), TAPS ** -0.5, 1.0, (), jnp.float32)
    basis_y = bell_draw(keys[8], (BASES, TAPS), TAPS ** -0.5, 1.0, (), jnp.float32)
    return {"exposures": exposures, "owners": owners, "offsets": offsets, "visit_shift": visit_shift, "visit_weight": visit_weight, "psf_class": psf_class, "coef_table": coef_table, "basis_x": basis_x, "basis_y": basis_y}


def lanczos_taps(fraction):
    distance = jnp.arange(6, dtype=jnp.int32).astype(jnp.float32) - 2.0 - fraction
    values = jnp.sinc(distance) * jnp.sinc(distance / 3.0)
    return values / jnp.sum(values)


def combined_taps(basis_rows, warp_x):
    summed = jnp.zeros((basis_rows.shape[0], basis_rows.shape[1] + 5), jnp.float32)
    for tap_slot in range(6):
        summed = summed + jnp.pad(basis_rows * warp_x[tap_slot], ((0, 0), (tap_slot, 5 - tap_slot)))
    return summed


def row_filter(slab_image, tap_values):
    row_count = slab_image.shape[0]
    width = slab_image.shape[1]
    blocks = width // 128
    padded = jnp.pad(slab_image, ((0, 0), (32, 96)))
    front_part = padded[:, :width].reshape(row_count, blocks, 128)
    second = padded[:, 128:width + 128].reshape(row_count, blocks, 128)[:, :, :64]
    windows = jnp.concatenate([front_part, second], axis=2)
    band_index = jnp.arange(192, dtype=jnp.int32)[:, None] - jnp.arange(128, dtype=jnp.int32)[None, :] - 15
    selector = (band_index[:, :, None] == jnp.arange(tap_values.shape[1], dtype=jnp.int32)[None, None, :]).astype(jnp.float32)
    band_matrix = jnp.einsum("aom,bm->bao", selector, tap_values.astype(jnp.float32), precision=lax.Precision.HIGHEST)
    band_matrix = band_matrix.astype(jnp.bfloat16)
    filtered = jnp.einsum("rna,bao->brno", windows.astype(jnp.float32), band_matrix.astype(jnp.float32), precision=lax.Precision.HIGHEST)
    return filtered.astype(jnp.bfloat16).reshape(tap_values.shape[0] * row_count, width)


def mixing(weight, coeffs, basis_y, row_count):
    tap_index = jnp.arange(row_count, dtype=jnp.int32)[None, :] - jnp.arange(row_count, dtype=jnp.int32)[:, None] + 15
    selector = (tap_index[:, :, None] == jnp.arange(basis_y.shape[1], dtype=jnp.int32)[None, None, :]).astype(jnp.float32)
    kernel_table = jnp.einsum("rsj,bj->rbs", selector, basis_y, precision=lax.Precision.HIGHEST)
    kernel_table = kernel_table * (weight * coeffs)[None, :, None]
    return kernel_table.astype(jnp.bfloat16).reshape(row_count, -1)


def reference(exposures, owners, offsets, visit_shift, visit_weight, psf_class, coef_table, basis_x, basis_y):
    row_ids = jnp.arange(STRIP_ROWS, dtype=jnp.int32)
    visit_items = (exposures.reshape(STEPS * N_STREAM, HOLD, STRIP_ROWS, COLS),
                   owners.reshape(STEPS * N_STREAM, HOLD, FANOUT),
                   offsets.reshape(STEPS * N_STREAM, HOLD, FANOUT),
                   visit_shift.reshape(STEPS * N_STREAM, 2),
                   visit_weight.reshape(STEPS * N_STREAM),
                   psf_class.reshape(STEPS * N_STREAM))

    def visit(coadd_sum, items):
        strips, owner_table, offset_table, shifts, weight, psf_index = items
        warp_x = lanczos_taps(shifts[0])
        warp_y = lanczos_taps(shifts[1])
        tap_index = row_ids[None, :] - row_ids[:, None] + 2
        ymat = jnp.sum((tap_index[:, :, None] == jnp.arange(6, dtype=jnp.int32)[None, None, :]).astype(jnp.float32) * warp_y, axis=2)
        ymat = ymat.astype(jnp.bfloat16)
        warped = jnp.einsum("ij,hjc->hic", ymat.astype(jnp.float32), strips.astype(jnp.float32), precision=lax.Precision.HIGHEST)
        slab_stack = jnp.zeros((N_PATCH * SLAB_ROWS, COLS), jnp.float32)
        for owner_slot in range(FANOUT):
            targets = (owner_table[:, owner_slot] * SLAB_ROWS + offset_table[:, owner_slot])[:, None] + row_ids[None, :]
            slab_stack = slab_stack.at[targets.reshape(-1)].add(warped.reshape(-1, COLS))
        slab_stack = slab_stack.astype(jnp.bfloat16).reshape(N_PATCH, SLAB_ROWS, COLS)
        tap_values = combined_taps(basis_x, warp_x).astype(jnp.bfloat16)
        class_hits = (psf_index == jnp.arange(CLASSES, dtype=jnp.int32)).astype(jnp.float32)
        coeffs = jnp.sum(class_hits[:, None] * coef_table, axis=0)
        mix_matrix = mixing(weight, coeffs, basis_y, SLAB_ROWS)

        def patch_term(slab_image):
            filtered = row_filter(slab_image, tap_values)
            return jnp.dot(mix_matrix.astype(jnp.float32), filtered.astype(jnp.float32), precision=lax.Precision.HIGHEST)

        terms = lax.map(patch_term, slab_stack)
        return coadd_sum + terms.reshape(N_PATCH * SLAB_ROWS, COLS), None

    coadd_sum, _ = lax.scan(visit, jnp.zeros((N_PATCH * SLAB_ROWS, COLS), jnp.float32), visit_items)
    return coadd_sum
```

```python
import functools

import jax
import jax.numpy as jnp
import numpy as np
from jax import lax
from jax.experimental import pallas as pl
from jax.experimental.pallas import tpu as pltpu
from jax.sharding import PartitionSpec as P

SLAB_ROWS = 64
ROWS = 8
TAPS_OUT = 36
CHUNKS = 4
SUB = 512
EMPTY = 128
VMEM_LIMIT = 58 * 1024 * 1024
HI = lax.Precision.HIGHEST


def lanczos_taps(fraction):
    distance = jnp.arange(6, dtype=jnp.int32).astype(jnp.float32) - 2.0 - fraction[..., None]
    values = jnp.sinc(distance) * jnp.sinc(distance / 3.0)
    return values / jnp.sum(values, axis=-1, keepdims=True)


def column_rows(basis_x, warp_x):
    summed = 0.0
    for q in range(6):
        part = basis_x[None, :, :] * warp_x[:, q, None, None]
        summed = summed + jnp.pad(part, ((0, 0), (0, 0), (q, 5 - q)))
    hx = summed.astype(jnp.bfloat16).astype(jnp.float32)
    return jnp.pad(hx[:, :, ::-1], ((0, 0), (0, 0), (206, 14)))


def row_table(weight, coeffs, basis_y, warp_y):
    steps, bases, taps = weight.shape[0], basis_y.shape[0], basis_y.shape[1]
    mix = basis_y[None] * (weight[:, None] * coeffs)[:, :, None]
    mix = mix.astype(jnp.bfloat16).astype(jnp.float32)
    i = np.arange(ROWS)
    tap = i[None, :] - i[:, None] + 2
    pick = (tap[:, :, None] == np.arange(6)).astype(np.float32)
    ymat = jnp.sum(pick[None] * warp_y[:, None, None, :], axis=3)
    ymat = ymat.astype(jnp.bfloat16).astype(jnp.float32)
    outer = mix.transpose(0, 2, 1)[:, :, None, :, None] * ymat[:, None, :, None, :]
    outer = outer.reshape(steps, taps * ROWS, bases * ROWS)
    u = np.arange(taps)
    place = (i[None, None, :] + 71 - u[None, :, None]) == np.arange(192)[:, None, None]
    place = place.astype(np.float32).reshape(192, taps * ROWS)
    return jnp.einsum("qk,tkn->tqn", place, outer, precision=HI)


def prep_kernel(streams, starts_ref, me_ref, v_ref, k2_ref, band_ref, w_ref):
    pairs = v_ref.shape[0] // 2
    patches = w_ref.shape[0]
    steps = k2_ref.shape[0]
    part = SLAB_ROWS // streams

    def one_band(g, c):
        for side in range(2):
            row = v_ref[pl.ds(g * 2 + side, 1), :]
            wide = jnp.broadcast_to(row, (256, 256))
            rolled = pltpu.roll(wide, 0, 1, stride=1, stride_axis=0)
            band_ref[g, :, side * 128 : (side + 1) * 128] = rolled[:, :128].astype(jnp.bfloat16)
        return c

    lax.fori_loop(0, pairs, one_band, 0)
    me = me_ref[0]

    def one_patch(q, c):
        for t in range(steps):
            for slot in range(2):
                base = starts_ref[(q * steps + t) * 2 + slot]
                rows = [
                    k2_ref[t, pl.ds(base + part * jnp.bitwise_xor(me, s), part), :]
                    for s in range(streams)
                ]
                block = jnp.concatenate(rows, axis=0).astype(jnp.bfloat16)
                w_ref[q, :, (t * 2 + slot) * 128 : (t * 2 + slot + 1) * 128] = block
        return c

    lax.fori_loop(0, patches, one_patch, 0)


def main_kernel(order, streams, strip_ref, x_ref, halo_ref, band_ref, w_ref, keep_ref, send_ref, f_ref):
    steps = x_ref.shape[0]
    strips = x_ref.shape[1] // ROWS
    patches = w_ref.shape[0]
    windows = SUB // 128
    part = SLAB_ROWS // streams

    for t in range(steps):
        pieces = []
        for n in range(windows):
            if n < windows - 1:
                pieces.append(x_ref[t, :, n * 128 : n * 128 + 256])
            else:
                pieces.append(jnp.concatenate([x_ref[t, :, n * 128 :], halo_ref[t]], axis=1))
        lhs = jnp.concatenate(pieces, axis=0)

        def one_pair(g, c):
            res = jnp.dot(lhs, band_ref[t * 8 + g], preferred_element_type=jnp.float32)
            res = res.reshape(windows, strips, ROWS, 256)
            for n in range(windows):
                two = jnp.concatenate([res[n, :, :, :128], res[n, :, :, 128:]], axis=1)
                f_ref[t * strips : (t + 1) * strips, g, :, n * 128 : (n + 1) * 128] = two.astype(jnp.bfloat16)
            return c

        lax.fori_loop(0, 8, one_pair, 0)

    bits = len(order)

    def one_patch(q, c):
        acc = jnp.zeros((SLAB_ROWS, SUB), jnp.float32)
        for t in range(steps):
            first = strip_ref[(q * steps + t) * 2]
            second = strip_ref[(q * steps + t) * 2 + 1]
            rhs = jnp.concatenate(
                [f_ref[first].reshape(128, SUB), f_ref[second].reshape(128, SUB)], axis=0
            )
            acc = acc + jnp.dot(
                w_ref[q, :, t * 256 : (t + 1) * 256], rhs, preferred_element_type=jnp.float32
            )
        pos = 0
        for place, bit in enumerate(order):
            pos = pos + (lax.shift_right_logical(q, bit) & 1) * (1 << (bits - 1 - place))
        for s in range(streams):
            rows = acc[s * part : (s + 1) * part]
            if s < streams // 2:
                keep_ref[s, pos] = rows
            else:
                send_ref[s - streams // 2, pos] = rows.astype(jnp.bfloat16)
        return c

    lax.fori_loop(0, patches, one_patch, 0)


def swap(x, axis, bit):
    n = lax.axis_size(axis)
    return lax.ppermute(x, axis, [(i, i ^ bit) for i in range(n)])


def shards(
    exposures, owners, offsets, visit_shift, visit_weight, psf_class, coef_table, basis_x, basis_y
):
    patches = lax.axis_size("patch")
    streams = lax.axis_size("stream")
    my_patch = lax.axis_index("patch")
    my_stream = lax.axis_index("stream")
    steps, strips, width = exposures.shape[0], exposures.shape[2], exposures.shape[4]
    part = SLAB_ROWS // streams
    patch_bits = patches.bit_length() - 1
    stream_bits = streams.bit_length() - 1

    x = exposures.reshape(steps, strips * ROWS, width)
    x = jnp.pad(x, ((0, 0), (0, 0), (32, 96)))

    warp = lanczos_taps(visit_shift[:, 0])
    vrows = column_rows(basis_x, warp[:, 0]).reshape(-1, 256)
    hits = (psf_class[:, 0, None] == jnp.arange(coef_table.shape[0], dtype=jnp.int32)).astype(jnp.float32)
    coeffs = jnp.sum(hits[:, :, None] * coef_table[None], axis=1)
    k2 = row_table(visit_weight[:, 0], coeffs, basis_y, warp[:, 1])

    wanted = jnp.bitwise_xor(jnp.arange(patches, dtype=jnp.int32), my_patch)
    own, off = owners[:, 0], offsets[:, 0]
    match = own[None] == wanted[:, None, None, None]
    named = jnp.any(match, axis=3)
    at = jnp.sum(jnp.where(match, off[None], 0), axis=3)
    ids = jnp.arange(strips, dtype=jnp.int32)
    first = jnp.min(jnp.where(named, ids, strips), axis=2)
    last = jnp.max(jnp.where(named, ids, -1), axis=2)
    one = named & (ids == first[..., None])
    two = named & (ids == last[..., None]) & (last > first)[..., None]
    start = jnp.stack(
        [jnp.sum(jnp.where(m, 56 - at - EMPTY, 0), axis=2) + EMPTY for m in (one, two)], axis=2
    )
    base = jnp.arange(steps, dtype=jnp.int32)[None] * strips
    strip = jnp.stack([base + jnp.clip(first, 0, strips - 1), base + jnp.clip(last, 0, strips - 1)], axis=2)
    start, strip = start.reshape(-1), strip.reshape(-1)

    smem = pl.BlockSpec(memory_space=pltpu.SMEM)
    vmem = pl.BlockSpec(memory_space=pltpu.VMEM)
    params = pltpu.CompilerParams(vmem_limit_bytes=VMEM_LIMIT)
    band, w = pl.pallas_call(
        functools.partial(prep_kernel, streams),
        out_shape=(
            jax.ShapeDtypeStruct((steps * 8, 256, 256), jnp.bfloat16),
            jax.ShapeDtypeStruct((patches, SLAB_ROWS, steps * 256), jnp.bfloat16),
        ),
        in_specs=[smem, smem, vmem, vmem],
        out_specs=(vmem, vmem),
        compiler_params=params,
    )(start, my_stream.reshape(1).astype(jnp.int32), vrows, k2)

    chunk = width // CHUNKS
    subs = chunk // SUB
    half = streams // 2
    flops = 2 * steps * strips * ROWS * chunk * 256 * 16 + 2 * patches * SLAB_ROWS * steps * 256 * chunk
    outs = []
    for c in range(CHUNKS):
        order = list(range(patch_bits))
        if c % 2 == 1:
            order[0], order[1] = order[1], order[0]
        first_sub = c * subs
        keep, send = pl.pallas_call(
            functools.partial(main_kernel, tuple(order), streams),
            grid_spec=pltpu.PrefetchScalarGridSpec(
                num_scalar_prefetch=1,
                grid=(subs,),
                in_specs=[
                    pl.BlockSpec((steps, strips * ROWS, SUB), lambda i, _, f=first_sub: (0, 0, f + i)),
                    pl.BlockSpec(
                        (steps, strips * ROWS, 128), lambda i, _, f=first_sub: (0, 0, (f + i + 1) * (SUB // 128))
                    ),
                    pl.BlockSpec(band.shape, lambda i, _: (0, 0, 0)),
                    pl.BlockSpec(w.shape, lambda i, _: (0, 0, 0)),
                ],
                out_specs=[
                    pl.BlockSpec((half, patches, part, SUB), lambda i, _: (0, 0, 0, i)),
                    pl.BlockSpec((half, patches, part, SUB), lambda i, _: (0, 0, 0, i)),
                ],
                scratch_shapes=[pltpu.VMEM((steps * strips, 8, 16, SUB), jnp.bfloat16)],
            ),
            out_shape=(
                jax.ShapeDtypeStruct((half, patches, part, chunk), jnp.float32),
                jax.ShapeDtypeStruct((half, patches, part, chunk), jnp.bfloat16),
            ),
            compiler_params=params,
            cost_estimate=pl.CostEstimate(flops=flops, bytes_accessed=12 << 20, transcendentals=0),
        )(strip, x, x, band, w)
        keep = keep.reshape(half * patches, part, chunk)
        send = send.reshape(half * patches, part, chunk)
        hops = [("stream", 1 << b) for b in reversed(range(stream_bits))]
        hops += [("patch", 1 << b) for b in order]
        for step, (axis, bit) in enumerate(hops):
            total = keep + swap(send, axis, bit).astype(jnp.float32)
            left = total.shape[0] // 2
            if step + 1 < len(hops):
                keep, send = total[:left], total[left:].astype(jnp.bfloat16)
        outs.append(total[0])
    return jnp.concatenate(outs, axis=1)


def solution(mesh):
    placed = (
        P(None, "stream", "patch", None, None),
        P(None, "stream", "patch", None),
        P(None, "stream", "patch", None),
        P(None, "stream", None),
        P(None, "stream"),
        P(None, "stream"),
        P(),
        P(),
        P(),
    )
    return jax.shard_map(
        shards, mesh=mesh, in_specs=placed, out_specs=P(("patch", "stream"), None), check_vma=False
    )
```

```python
import functools

import jax
import jax.numpy as jnp
import numpy as np
from jax import lax
from jax.experimental import pallas as pl
from jax.experimental.pallas import tpu as pltpu
from jax.sharding import PartitionSpec as P

SLAB_ROWS = 64
ROWS = 8
TAPS_OUT = 36
CHUNKS = 4
EMPTY = 128
VMEM_LIMIT = 42 * 1024 * 1024
HI = lax.Precision.HIGHEST


def lanczos_taps(fraction):
    distance = jnp.arange(6, dtype=jnp.int32).astype(jnp.float32) - 2.0 - fraction[..., None]
    values = jnp.sinc(distance) * jnp.sinc(distance / 3.0)
    return values / jnp.sum(values, axis=-1, keepdims=True)


def column_rows(basis_x, warp_x):
    summed = 0.0
    for q in range(6):
        part = basis_x[None, :, :] * warp_x[:, q, None, None]
        summed = summed + jnp.pad(part, ((0, 0), (0, 0), (q, 5 - q)))
    hx = summed.astype(jnp.bfloat16).astype(jnp.float32)
    return jnp.pad(hx[:, :, ::-1], ((0, 0), (0, 0), (206, 14)))


def row_table(weight, coeffs, basis_y, warp_y):
    bases, taps = basis_y.shape
    mix = basis_y[None] * (weight[:, None] * coeffs)[:, :, None]
    mix = mix.astype(jnp.bfloat16).astype(jnp.float32)
    i = np.arange(ROWS)
    tap = i[None, :] - i[:, None] + 2
    pick = (tap[:, :, None] == np.arange(6)).astype(np.float32)
    ymat = jnp.sum(pick[None] * warp_y[:, None, None, :], axis=3)
    ymat = ymat.astype(jnp.bfloat16).astype(jnp.float32)
    rows = jnp.repeat(mix[:, :, ::-1].transpose(0, 2, 1), ROWS, axis=2)
    lanes = jnp.tile(ymat, (1, 1, bases))
    table = 0.0
    for k in range(ROWS):
        placed = jnp.pad(rows, ((0, 0), (41 + k, 192 - taps - 41 - k), (0, 0)))
        table = table + placed * lanes[:, k : k + 1]
    return table


def prep_kernel(streams, starts_ref, me_ref, v_ref, k2_ref, band_ref, w_ref):
    pairs = v_ref.shape[0] // 2
    patches = w_ref.shape[0]
    steps = k2_ref.shape[0]
    part = SLAB_ROWS // streams

    def one_band(g, c):
        for side in range(2):
            row = v_ref[pl.ds(g * 2 + side, 1), :]
            wide = jnp.broadcast_to(row, (256, 256))
            rolled = pltpu.roll(wide, 0, 1, stride=1, stride_axis=0)
            band_ref[g, :, side * 128 : (side + 1) * 128] = rolled[:, :128].astype(jnp.bfloat16)
        return c

    lax.fori_loop(0, pairs, one_band, 0)
    me = me_ref[0]

    def one_patch(q, c):
        for t in range(steps):
            for slot in range(2):
                base = starts_ref[(q * steps + t) * 2 + slot]
                rows = [
                    k2_ref[t, pl.ds(base + part * jnp.bitwise_xor(me, s), part), :]
                    for s in range(streams)
                ]
                block = jnp.concatenate(rows, axis=0).astype(jnp.bfloat16)
                w_ref[q, :, (t * 2 + slot) * 128 : (t * 2 + slot + 1) * 128] = block
        return c

    lax.fori_loop(0, patches, one_patch, 0)


def field_sizes(bits):
    sizes = [2] * (bits // 2)
    return sizes + [1] * (bits % 2)


def main_kernel(first_block, blocks, patch_bits, streams, strip_ref, x_ref, band_ref, w_ref, keep_ref, send_ref, f_ref):
    steps = x_ref.shape[0]
    strips = x_ref.shape[1] // ROWS
    tiles = x_ref.shape[2] // 128
    patches = w_ref.shape[0]
    part = SLAB_ROWS // streams
    width = blocks * 128

    def one_step(t, c):
        pieces = []
        for n in range(first_block, first_block + blocks):
            if 0 <= n and n + 2 <= tiles:
                pieces.append(x_ref[t, :, n * 128 : n * 128 + 256])
            else:
                blank = jnp.zeros((strips * ROWS, 128), jnp.bfloat16)
                sides = [x_ref[t, :, m * 128 : (m + 1) * 128] if 0 <= m < tiles else blank for m in (n, n + 1)]
                pieces.append(jnp.concatenate(sides, axis=1))
        lhs = jnp.concatenate(pieces, axis=0)
        for g in range(8):
            res = jnp.dot(lhs, band_ref[t * 8 + g], preferred_element_type=jnp.float32)
            res = res.reshape(blocks, strips, ROWS, 256)
            for n in range(blocks):
                two = jnp.concatenate([res[n, :, :, :128], res[n, :, :, 128:]], axis=1)
                f_ref[pl.ds(t * strips, strips), g, :, n * 128 : (n + 1) * 128] = two.astype(jnp.bfloat16)
        return c

    lax.fori_loop(0, steps, one_step, 0)

    def one_patch(q):
        rhs = jnp.concatenate(
            [f_ref[strip_ref[q * steps * 2 + k]].reshape(128, width) for k in range(2 * steps)], axis=0
        )
        acc = jnp.dot(w_ref[q], rhs, preferred_element_type=jnp.float32)
        pos, low, left = 0, 0, patches
        for size in field_sizes(patch_bits):
            left = left >> size
            pos = pos + (lax.shift_right_logical(q, low) & ((1 << size) - 1)) * left
            low += size
        keep_ref[pos] = acc[:part]
        for s in range(1, streams):
            send_ref[s - 1, pos] = acc[s * part : (s + 1) * part].astype(jnp.bfloat16)

    def four(i, c):
        for k in range(4):
            one_patch(i * 4 + k)
        return c

    lax.fori_loop(0, patches // 4, four, 0)


def swap(x, axis, mask):
    n = lax.axis_size(axis)
    return lax.ppermute(x, axis, [(i, i ^ mask) for i in range(n)])


def add_all(keep, arrived):
    for one in arrived:
        keep = keep + one.astype(jnp.float32)
    return keep


def shards(
    exposures, owners, offsets, visit_shift, visit_weight, psf_class, coef_table, basis_x, basis_y
):
    patches = lax.axis_size("patch")
    streams = lax.axis_size("stream")
    my_patch = lax.axis_index("patch")
    my_stream = lax.axis_index("stream")
    steps, strips, width = exposures.shape[0], exposures.shape[2], exposures.shape[4]
    part = SLAB_ROWS // streams
    patch_bits = patches.bit_length() - 1

    x = exposures.reshape(steps, strips * ROWS, width)

    warp = lanczos_taps(visit_shift[:, 0])
    vrows = column_rows(basis_x, warp[:, 0]).reshape(-1, 256)
    hits = (psf_class[:, 0, None] == jnp.arange(coef_table.shape[0], dtype=jnp.int32)).astype(jnp.float32)
    coeffs = jnp.sum(hits[:, :, None] * coef_table[None], axis=1)
    k2 = row_table(visit_weight[:, 0], coeffs, basis_y, warp[:, 1])

    wanted = jnp.bitwise_xor(jnp.arange(patches, dtype=jnp.int32), my_patch)
    own, off = owners[:, 0], offsets[:, 0]
    match = own[None] == wanted[:, None, None, None]
    named = jnp.any(match, axis=3)
    at = jnp.sum(jnp.where(match, off[None], 0), axis=3)
    ids = jnp.arange(strips, dtype=jnp.int32)
    first = jnp.min(jnp.where(named, ids, strips), axis=2)
    last = jnp.max(jnp.where(named, ids, -1), axis=2)
    one = named & (ids == first[..., None])
    two = named & (ids == last[..., None]) & (last > first)[..., None]
    start = jnp.stack(
        [jnp.sum(jnp.where(m, 56 - at - EMPTY, 0), axis=2) + EMPTY for m in (one, two)], axis=2
    )
    base = jnp.arange(steps, dtype=jnp.int32)[None] * strips
    strip = jnp.stack([base + jnp.clip(first, 0, strips - 1), base + jnp.clip(last, 0, strips - 1)], axis=2)
    start, strip = start.reshape(-1), strip.reshape(-1)

    smem = pl.BlockSpec(memory_space=pltpu.SMEM)
    vmem = pl.BlockSpec(memory_space=pltpu.VMEM)
    params = pltpu.CompilerParams(vmem_limit_bytes=VMEM_LIMIT)
    band, w = pl.pallas_call(
        functools.partial(prep_kernel, streams),
        out_shape=(
            jax.ShapeDtypeStruct((steps * 8, 256, 256), jnp.bfloat16),
            jax.ShapeDtypeStruct((patches, SLAB_ROWS, steps * 256), jnp.bfloat16),
        ),
        in_specs=[smem, smem, vmem, vmem],
        out_specs=(vmem, vmem),
        compiler_params=params,
    )(start, my_stream.reshape(1).astype(jnp.int32), vrows, k2)

    total_blocks = width // 128 + 1
    sizes = [total_blocks // CHUNKS + (c < total_blocks % CHUNKS) for c in range(CHUNKS)]
    fields = field_sizes(patch_bits)

    def hop(total, k):
        low = sum(fields[:k])
        parts = total.reshape(1 << fields[k], -1, part, total.shape[-1])
        sends = [parts[g].astype(jnp.bfloat16) for g in range(1, 1 << fields[k])]
        return add_all(parts[0], [swap(v, "patch", (g + 1) << low) for g, v in enumerate(sends)])

    sums = []
    begin = -1
    for c, blocks in enumerate(sizes):
        wide = blocks * 128
        table = strip
        if c >= 2:
            table, *tied = lax.optimization_barrier((strip, *sums[max(0, c - 1 - len(fields)) : c - 1]))
            for k, total in enumerate(reversed(tied)):
                sums[c - 2 - k] = hop(total, k)
        keep, send = pl.pallas_call(
            functools.partial(main_kernel, begin, blocks, patch_bits, streams),
            in_specs=[smem, vmem, vmem, vmem],
            out_specs=(vmem, vmem),
            out_shape=(
                jax.ShapeDtypeStruct((patches, part, wide), jnp.float32),
                jax.ShapeDtypeStruct((streams - 1, patches, part, wide), jnp.bfloat16),
            ),
            scratch_shapes=[pltpu.VMEM((steps * strips, 8, 16, wide), jnp.bfloat16)],
            compiler_params=params,
            cost_estimate=pl.CostEstimate(flops=12 << 30, bytes_accessed=12 << 20, transcendentals=0),
        )(table, x, band, w)
        begin += blocks
        sums.append(add_all(keep, [swap(send[s - 1], "stream", s) for s in range(1, streams)]))
    for c in range(CHUNKS):
        for k in range(min(len(fields), max(0, CHUNKS - 2 - c + 0)), len(fields)):
            sums[c] = hop(sums[c], k)
    out = jnp.concatenate([total[0] for total in sums], axis=1)
    return out[:, 96 : 96 + width]


def solution(mesh):
    placed = (
        P(None, "stream", "patch", None, None),
        P(None, "stream", "patch", None),
        P(None, "stream", "patch", None),
        P(None, "stream", None),
        P(None, "stream"),
        P(None, "stream"),
        P(),
        P(),
        P(),
    )
    return jax.shard_map(
        shards, mesh=mesh, in_specs=placed, out_specs=P(("patch", "stream"), None), check_vma=False
    )
```

```python
import functools

import jax
import jax.numpy as jnp
import numpy as np
from jax import lax
from jax.experimental import pallas as pl
from jax.experimental.pallas import tpu as pltpu
from jax.sharding import PartitionSpec as P

SLAB_ROWS = 64
ROWS = 8
TAPS_OUT = 36
BLOCKS = 3
EMPTY = 128
VMEM_LIMIT = 58 * 1024 * 1024
HI = lax.Precision.HIGHEST


def lanczos_taps(fraction):
    distance = jnp.arange(6, dtype=jnp.int32).astype(jnp.float32) - 2.0 - fraction[..., None]
    values = jnp.sinc(distance) * jnp.sinc(distance / 3.0)
    return values / jnp.sum(values, axis=-1, keepdims=True)


def column_rows(basis_x, warp_x):
    summed = 0.0
    for q in range(6):
        part = basis_x[None, :, :] * warp_x[:, q, None, None]
        summed = summed + jnp.pad(part, ((0, 0), (0, 0), (q, 5 - q)))
    hx = summed.astype(jnp.bfloat16).astype(jnp.float32)
    return jnp.pad(hx[:, :, ::-1], ((0, 0), (0, 0), (206, 14)))


def row_table(weight, coeffs, basis_y, warp_y):
    bases, taps = basis_y.shape
    mix = basis_y[None] * (weight[:, None] * coeffs)[:, :, None]
    mix = mix.astype(jnp.bfloat16).astype(jnp.float32)
    i = np.arange(ROWS)
    tap = i[None, :] - i[:, None] + 2
    pick = (tap[:, :, None] == np.arange(6)).astype(np.float32)
    ymat = jnp.sum(pick[None] * warp_y[:, None, None, :], axis=3)
    ymat = ymat.astype(jnp.bfloat16).astype(jnp.float32)
    rows = jnp.repeat(mix[:, :, ::-1].transpose(0, 2, 1), ROWS, axis=2)
    lanes = jnp.tile(ymat, (1, 1, bases))
    table = 0.0
    for k in range(ROWS):
        placed = jnp.pad(rows, ((0, 0), (41 + k, 192 - taps - 41 - k), (0, 0)))
        table = table + placed * lanes[:, k : k + 1]
    return table


def prep_kernel(streams, starts_ref, me_ref, v_ref, k2_ref, band_ref, w_ref):
    pairs = v_ref.shape[0] // 2
    patches = w_ref.shape[0]
    steps = k2_ref.shape[0]
    part = SLAB_ROWS // streams

    def one_band(g, c):
        for side in range(2):
            row = v_ref[pl.ds(g * 2 + side, 1), :]
            wide = jnp.broadcast_to(row, (256, 256))
            rolled = pltpu.roll(wide, 0, 1, stride=1, stride_axis=0)
            band_ref[g, :, side * 128 : (side + 1) * 128] = rolled[:, :128].astype(jnp.bfloat16)
        return c

    lax.fori_loop(0, pairs, one_band, 0)
    me = me_ref[0]

    def one_patch(q, c):
        for t in range(steps):
            for slot in range(2):
                base = starts_ref[(q * steps + t) * 2 + slot]
                rows = [
                    k2_ref[t, pl.ds(base + part * jnp.bitwise_xor(me, s), part), :]
                    for s in range(streams)
                ]
                block = jnp.concatenate(rows, axis=0).astype(jnp.bfloat16)
                w_ref[q, :, (t * 2 + slot) * 128 : (t * 2 + slot + 1) * 128] = block
        return c

    lax.fori_loop(0, patches, one_patch, 0)


def partner(me, mask):
    other, bit = me, 1
    while bit <= mask:
        if mask & bit:
            other = other + bit * (1 - 2 * ((me // bit) % 2))
        bit *= 2
    return other


def fused_kernel(
    strip_ref, x_ref, band_ref, w_ref, out_ref,
    f_ref, keep0, keep1, keep2, out0, out1, out2, in0, in1, in2, *sems
):
    steps = x_ref.shape[0]
    strips = x_ref.shape[1] // ROWS
    patches = w_ref.shape[0]
    chunks, part, width = out_ref.shape
    streams = SLAB_ROWS // part
    fields = [1 << 2, patches >> 2]
    my_patch, my_stream = lax.axis_index("patch"), lax.axis_index("stream")
    peers = [
        [{"stream": partner(my_stream, g)} for g in range(1, streams)],
        [{"patch": partner(my_patch, g)} for g in range(1, fields[0])],
        [{"patch": partner(my_patch, g * fields[0])} for g in range(1, fields[1])],
    ]
    outs, ins = (out0, out1, out2), (in0, in1, in2)
    gone, come = sems[:3], sems[3:]

    barrier = pltpu.get_barrier_semaphore()
    for group in peers:
        for device in group:
            pl.semaphore_signal(barrier, inc=1, device_id=device, device_id_type=pl.DeviceIdType.MESH)
    pl.semaphore_wait(barrier, sum(len(group) for group in peers))

    def copy(k, c, g):
        return pltpu.make_async_remote_copy(
            src_ref=outs[k].at[c, g],
            dst_ref=ins[k].at[c, g],
            send_sem=gone[k].at[c, g],
            recv_sem=come[k].at[c, g],
            device_id=peers[k][g],
            device_id_type=pl.DeviceIdType.MESH,
        )

    def compute(c):
        def one_step(t, carry):
            pieces = [
                x_ref[t, :, pl.ds(pl.multiple_of((c * BLOCKS + n) * 128, 128), 256)] for n in range(BLOCKS)
            ]
            lhs = jnp.concatenate(pieces, axis=0)
            for g in range(8):
                res = jnp.dot(lhs, band_ref[t * 8 + g], preferred_element_type=jnp.float32)
                res = res.reshape(BLOCKS, strips, ROWS, 256)
                for n in range(BLOCKS):
                    two = jnp.concatenate([res[n, :, :, :128], res[n, :, :, 128:]], axis=1)
                    f_ref[pl.ds(t * strips, strips), g, :, n * 128 : (n + 1) * 128] = two.astype(jnp.bfloat16)
            return carry

        lax.fori_loop(0, steps, one_step, 0)

        def four(i, carry):
            for k in range(fields[0]):
                q = i * fields[0] + k
                rhs = jnp.concatenate(
                    [f_ref[strip_ref[q * steps * 2 + m]].reshape(128, width) for m in range(2 * steps)], axis=0
                )
                acc = jnp.dot(w_ref[q], rhs, preferred_element_type=jnp.float32)
                pos = k * fields[1] + i
                keep0[c % 2, pos] = acc[:part]
                for s in range(1, streams):
                    out0[c, s - 1, pos] = acc[s * part : (s + 1) * part].astype(jnp.bfloat16)
            return carry

        lax.fori_loop(0, fields[1], four, 0)

    def arrive(k, c):
        for g in range(len(peers[k])):
            copy(k, c, g).wait_recv()

    def send(k, c):
        for g in range(len(peers[k])):
            copy(k, c, g).start()

    def slot(i, carry):
        @pl.when(i < chunks)
        def _():
            compute(i)
            send(0, i)

        @pl.when(i >= 3)
        def _():
            c = i - 3
            arrive(2, c)
            total = keep2[...]
            for g in range(len(peers[2])):
                total = total + in2[c, g, 0].astype(jnp.float32)
            out_ref[c] = total

        @pl.when((i >= 2) & (i < chunks + 2))
        def _():
            c = i - 2
            arrive(1, c)

            def one(z):
                total = keep1[z]
                for g in range(len(peers[1])):
                    total = total + in1[c, g, z].astype(jnp.float32)
                return total

            keep2[...] = one(0)
            for z in range(1, fields[1]):
                out2[c, z - 1, 0] = one(z).astype(jnp.bfloat16)
            send(2, c)

        @pl.when((i >= 1) & (i < chunks + 1))
        def _():
            c = i - 1
            arrive(0, c)

            def one(z, carry):
                for k in range(fields[0]):
                    pos = k * fields[1] + z
                    total = keep0[c % 2, pos]
                    for g in range(len(peers[0])):
                        total = total + in0[c, g, pos].astype(jnp.float32)
                    if k == 0:
                        keep1[z] = total
                    else:
                        out1[c, k - 1, z] = total.astype(jnp.bfloat16)
                return carry

            lax.fori_loop(0, fields[1], one, 0)
            send(1, c)

        return carry

    lax.fori_loop(0, chunks + 3, slot, 0)

    def leave(c, carry):
        for k in range(3):
            for g in range(len(peers[k])):
                copy(k, c, g).wait_send()
        return carry

    lax.fori_loop(0, chunks, leave, 0)


def shards(
    exposures, owners, offsets, visit_shift, visit_weight, psf_class, coef_table, basis_x, basis_y
):
    patches = lax.axis_size("patch")
    streams = lax.axis_size("stream")
    my_patch = lax.axis_index("patch")
    my_stream = lax.axis_index("stream")
    steps, strips, width = exposures.shape[0], exposures.shape[2], exposures.shape[4]
    part = SLAB_ROWS // streams
    chunks = -(-(width // 128 + 1) // BLOCKS)
    wide = BLOCKS * 128
    padded = chunks * wide - width

    x = jnp.pad(exposures.reshape(steps, strips * ROWS, width), ((0, 0), (0, 0), (128, padded)))

    warp = lanczos_taps(visit_shift[:, 0])
    vrows = column_rows(basis_x, warp[:, 0]).reshape(-1, 256)
    hits = (psf_class[:, 0, None] == jnp.arange(coef_table.shape[0], dtype=jnp.int32)).astype(jnp.float32)
    coeffs = jnp.sum(hits[:, :, None] * coef_table[None], axis=1)
    k2 = row_table(visit_weight[:, 0], coeffs, basis_y, warp[:, 1])

    wanted = jnp.bitwise_xor(jnp.arange(patches, dtype=jnp.int32), my_patch)
    own, off = owners[:, 0], offsets[:, 0]
    match = own[None] == wanted[:, None, None, None]
    named = jnp.any(match, axis=3)
    at = jnp.sum(jnp.where(match, off[None], 0), axis=3)
    ids = jnp.arange(strips, dtype=jnp.int32)
    first = jnp.min(jnp.where(named, ids, strips), axis=2)
    last = jnp.max(jnp.where(named, ids, -1), axis=2)
    one = named & (ids == first[..., None])
    two = named & (ids == last[..., None]) & (last > first)[..., None]
    start = jnp.stack(
        [jnp.sum(jnp.where(m, 56 - at - EMPTY, 0), axis=2) + EMPTY for m in (one, two)], axis=2
    )
    base = jnp.arange(steps, dtype=jnp.int32)[None] * strips
    strip = jnp.stack([base + jnp.clip(first, 0, strips - 1), base + jnp.clip(last, 0, strips - 1)], axis=2)
    start, strip = start.reshape(-1), strip.reshape(-1)

    smem = pl.BlockSpec(memory_space=pltpu.SMEM)
    vmem = pl.BlockSpec(memory_space=pltpu.VMEM)
    params = pltpu.CompilerParams(vmem_limit_bytes=VMEM_LIMIT)
    band, w = pl.pallas_call(
        functools.partial(prep_kernel, streams),
        out_shape=(
            jax.ShapeDtypeStruct((steps * 8, 256, 256), jnp.bfloat16),
            jax.ShapeDtypeStruct((patches, SLAB_ROWS, steps * 256), jnp.bfloat16),
        ),
        in_specs=[smem, smem, vmem, vmem],
        out_specs=(vmem, vmem),
        compiler_params=params,
    )(start, my_stream.reshape(1).astype(jnp.int32), vrows, k2)

    near, far = 4, patches // 4
    bf16, f32 = jnp.bfloat16, jnp.float32
    shapes = [(streams - 1, patches), (near - 1, far), (far - 1, 1)]
    buffers = [pltpu.VMEM((chunks, n, m, part, wide), bf16) for n, m in shapes]
    sems = [pltpu.SemaphoreType.DMA((chunks, n)) for n, m in shapes]
    out = pl.pallas_call(
        fused_kernel,
        in_specs=[smem, vmem, vmem, vmem],
        out_specs=vmem,
        out_shape=jax.ShapeDtypeStruct((chunks, part, wide), f32),
        scratch_shapes=[
            pltpu.VMEM((steps * strips, 8, 16, wide), bf16),
            pltpu.VMEM((2, patches, part, wide), f32),
            pltpu.VMEM((far, part, wide), f32),
            pltpu.VMEM((part, wide), f32),
            *buffers,
            *buffers,
            *sems,
            *sems,
        ],
        compiler_params=pltpu.CompilerParams(
            vmem_limit_bytes=VMEM_LIMIT, collective_id=0, has_side_effects=True
        ),
        cost_estimate=pl.CostEstimate(flops=30 << 30, bytes_accessed=12 << 20, transcendentals=0),
    )(strip, x, band, w)
    out = out.transpose(1, 0, 2).reshape(part, chunks * wide)
    return out[:, 96 : 96 + width]


def solution(mesh):
    placed = (
        P(None, "stream", "patch", None, None),
        P(None, "stream", "patch", None),
        P(None, "stream", "patch", None),
        P(None, "stream", None),
        P(None, "stream"),
        P(None, "stream"),
        P(),
        P(),
        P(),
    )
    return jax.shard_map(
        shards, mesh=mesh, in_specs=placed, out_specs=P(("patch", "stream"), None), check_vma=False
    )
```
